32 devices in a mesh: gz: 8 (over z, y), gy: 4 (over x, core).
Axes of the slice: x: 2, y: 2, z: 4, core: 2. Of those that a mesh axis runs over, the one named last changes fastest.
Arguments:
- patch_force: float32 [4096, 24, 128], P(('gz', 'gy')), may hold values from -36 to 36
- patch_owner: int32 [4096], P(('gz', 'gy')), may hold values from 0 to 31, as said below
- patch_voxel: int32 [4096, 128], P(('gz', 'gy')), may hold values from 0 to 16383
- patch_live: int32 [4096, 8], P(('gz', 'gy')), may hold values from 64 to 128
- voxel_mask: int32 [64, 32, 256], P('gz', 'gy'), may hold values 0 or 1
- element_matrix: float32 [24, 24], replicated, may hold values from -0.2 to 6.5, as said below
Outputs:
- displacement: float32 [24, 64, 32, 256], P(None, 'gz', 'gy')
- residual: float32 [24, 64, 32, 256], P(None, 'gz', 'gy')
The draws below stay inside these ranges and needn't reach their ends.
Inputs may be any that keep to these rules, and one draw needn't show every extreme that they name: `patch_owner`: within the 128 patch blocks of one device no owner appears more than 8 times, and in every device's blocks some owner appears exactly 8 times. `element_matrix`: symmetric positive definite.
All inputs are finite; a program needn't handle non-finite values. No bound on the sum of `voxel_mask` on one device may be relied on, other than what follows from the above.
Results may differ from the reference program's by a relative error of at most 0.00029.
Values sent between devices are 32-bit elements; how exact they have to be, the bound alone decides.
A program may use at most 128 MiB of HBM per device.

```python
import math
import jax
import jax.numpy as jnp
from jax import lax

CZ = 8
CY = 8
NX = 256
LOADS = 8
PS = 128
PATCH_DEV = 128
ITERS = 2
NZ = 64
NY = 32
PATCHES = 4096
CAP = 8
N_GZ = 8
N_GY = 4
DEVICES = 32


def draw_patch_owner(key, part):
    slot_total = DEVICES * CAP

    def one_block(block_index):
        block_key = jax.random.fold_in(jax.random.fold_in(key, 11), block_index)
        key_base, key_pick, key_order = jax.random.split(block_key, 3)
        slot_index = jnp.arange(slot_total, dtype=jnp.int32)
        owner_of = slot_index // CAP
        level = owner_of // N_GY
        base_score = jax.random.randint(key_base, (slot_total,), 0, 1024, dtype=jnp.int32)
        favored = jax.random.randint(key_pick, (), 0, DEVICES, dtype=jnp.int32)
        score = base_score + 300 * level // max(N_GZ - 1, 1) + jnp.where(owner_of == favored, 1 << 20, 0)
        score = score * slot_total + slot_index
        ignored, picked = lax.top_k(score, PATCH_DEV)
        shuffle = jax.random.permutation(key_order, PATCH_DEV)
        return (picked[shuffle] // CAP).astype(jnp.int32)
    owners = jax.vmap(one_block)(jnp.arange(DEVICES, dtype=jnp.int32))
    return owners.reshape(-1)


def draw_patch_live(key, part):
    key_main, key_row, key_col = jax.random.split(jax.random.fold_in(key, 23), 3)
    counts = jax.random.randint(key_main, (PATCHES, LOADS), PS // 2, PS + 1, dtype=jnp.int32)
    row_pick = jax.random.randint(key_row, (), 0, PATCHES, dtype=jnp.int32)
    col_pick = jax.random.randint(key_col, (), 0, LOADS, dtype=jnp.int32)
    return counts.at[row_pick, col_pick].set(PS)


def draw_patch_force(key, part):
    key_patch, key_chan, key_base = jax.random.split(jax.random.fold_in(key, 37), 3)
    patch_scale = jnp.exp(jax.random.uniform(key_patch, (PATCHES, 1, 1), jnp.float32, math.log(0.3), math.log(3.0)))
    chan_scale = jnp.exp(jax.random.uniform(key_chan, (1, 3 * LOADS, 1), jnp.float32, math.log(0.5), math.log(2.0)))
    base_value = jnp.clip(jax.random.normal(key_base, (PATCHES, 3 * LOADS, PS), jnp.float32), -6.0, 6.0)
    return base_value * patch_scale * chan_scale


def draw_element_matrix(key, part):
    key_off, key_diag = jax.random.split(jax.random.fold_in(key, 41), 2)
    raw_off = jax.random.uniform(key_off, (24, 24), jnp.float32, -0.2, 0.2)
    symmetric = 0.5 * (raw_off + raw_off.T)
    identity = jnp.eye(24, dtype=jnp.float32)
    off_part = symmetric * (1.0 - identity)
    row_weight = jnp.sum(jnp.abs(off_part), axis=1)
    diag_part = 1.25 * row_weight + jax.random.uniform(key_diag, (24,), jnp.float32, 0.2, 0.6)
    return off_part + identity * diag_part[None, :]


def with_ends(result, stream_key, low, top_value):
    longest = result.shape.index(max(result.shape))
    spots = []
    for shift in (0, 1):
        where = [jax.random.randint(jax.random.fold_in(stream_key, axis), (), 0, length) for axis, length in enumerate(result.shape)]
        where[longest] = (where[longest] + shift) % result.shape[longest]
        spots.append(tuple(where))
    return result.at[spots[0]].set(low).at[spots[1]].set(top_value)


def setup_inputs(seed: int = 0) -> dict:
    arg_keys = jax.random.split(jax.random.key(seed), 7)
    patch_force = draw_patch_force(jax.random.fold_in(arg_keys[6], 71), 0)
    patch_owner = draw_patch_owner(jax.random.fold_in(arg_keys[6], 71), 0)
    patch_voxel = with_ends(jax.random.randint(arg_keys[2], (PATCHES, PS), 0, CZ * CY * NX), jax.random.fold_in(arg_keys[2], 1), 0, (CZ * CY * NX) - 1).astype(jnp.int32)
    patch_live = draw_patch_live(jax.random.fold_in(arg_keys[6], 71), 0)
    voxel_mask = with_ends((jax.random.randint(arg_keys[4], (NZ, NY, NX), 0, 2) < 1).astype(jnp.int32), jax.random.fold_in(arg_keys[4], 1), 0, 1)
    element_matrix = draw_element_matrix(jax.random.fold_in(arg_keys[6], 71), 0)
    return dict(patch_force=patch_force, patch_owner=patch_owner, patch_voxel=patch_voxel, patch_live=patch_live, voxel_mask=voxel_mask, element_matrix=element_matrix)


spring = 0.5
highest = lax.Precision.HIGHEST

def plane_terms(padded, modulus, element_matrix, plane_index):
    load_count = padded.shape[0] // 3
    width_rows = padded.shape[2] - 2
    width_cols = padded.shape[3] - 2
    layer = lax.dynamic_slice_in_dim(padded, plane_index, 2, 1)
    corners = []
    for corner_z in (0, 1):
        for corner_y in (0, 1):
            for corner_x in (0, 1):
                corners.append(layer[:, corner_z, corner_y:corner_y + width_rows + 1, corner_x:corner_x + width_cols + 1])
    stacked = jnp.stack(corners, 0).reshape(24, load_count, -1)
    weights = lax.dynamic_index_in_dim(modulus, plane_index, 0, False).reshape(1, 1, -1)
    forces = jnp.einsum('ij,jlq->ilq', element_matrix, stacked, precision=highest) * weights
    forces = forces.reshape(8, 3 * load_count, width_rows + 1, width_cols + 1)
    lower_part = jnp.zeros((3 * load_count, width_rows, width_cols), forces.dtype)
    upper_part = jnp.zeros((3 * load_count, width_rows, width_cols), forces.dtype)
    for corner_y in (0, 1):
        for corner_x in (0, 1):
            start_y = 1 - corner_y
            start_x = 1 - corner_x
            lower_part = lower_part + forces[corner_y * 2 + corner_x][:, start_y:start_y + width_rows, start_x:start_x + width_cols]
            upper_part = upper_part + forces[4 + corner_y * 2 + corner_x][:, start_y:start_y + width_rows, start_x:start_x + width_cols]
    return (lower_part, upper_part)

def assemble(padded, modulus, element_matrix):
    plane_count = modulus.shape[0]
    lower_part, upper_part = lax.map(lambda plane_index: plane_terms(padded, modulus, element_matrix, plane_index), jnp.arange(plane_count, dtype=jnp.int32))
    combined = lower_part[1:] + upper_part[:-1]
    return jnp.transpose(combined, (1, 0, 2, 3))

def gram_local(first, second):
    return jnp.einsum('clq,cmq->lm', first.reshape(3, LOADS, -1), second.reshape(3, LOADS, -1), precision=highest)

def combine(vector_field, matrix):
    mixed = jnp.einsum('clq,lm->cmq', vector_field.reshape(3, LOADS, -1), matrix, precision=highest)
    return mixed.reshape(vector_field.shape)

def solve_small(matrix, target):
    factor = jnp.linalg.cholesky(matrix)
    halfway = lax.linalg.triangular_solve(factor, target, left_side=True, lower=True)
    return lax.linalg.triangular_solve(factor, halfway, left_side=True, lower=True, transpose_a=True)

def reference(patch_force, patch_owner, patch_voxel, patch_live, voxel_mask, element_matrix):
    channels = 3 * LOADS
    owner_z = (patch_owner // N_GY)[:, None]
    owner_y = (patch_owner % N_GY)[:, None]
    coord_z = owner_z * CZ + patch_voxel // (CY * NX)
    coord_y = owner_y * CY + patch_voxel // NX % CY
    coord_x = patch_voxel % NX
    flat_ids = ((coord_z * NY + coord_y) * NX + coord_x).reshape(-1).astype(jnp.int32)
    load_of = jnp.arange(channels, dtype=jnp.int32) % LOADS
    live_count = patch_live[:, load_of]
    keep = jnp.arange(PS, dtype=jnp.int32)[None, None, :] < live_count[:, :, None]
    loaded = jnp.where(keep, patch_force, jnp.zeros_like(patch_force))
    contrib = jnp.transpose(loaded, (1, 0, 2)).reshape(channels, -1)
    nodal_force = jnp.zeros((channels, NZ * NY * NX), patch_force.dtype).at[:, flat_ids].add(contrib)
    nodal_force = nodal_force.reshape(channels, NZ, NY, NX)
    modulus = jnp.pad(voxel_mask.astype(patch_force.dtype), ((1, 0), (1, 0), (1, 0)))
    modulus = modulus.reshape(NZ + 1, (NY + 1) * (NX + 1))

    def apply_operator(vector_field):
        padded = jnp.pad(vector_field, ((0, 0), (1, 1), (1, 1), (1, 1)))
        return assemble(padded, modulus, element_matrix) + spring * vector_field
    displacement = jnp.zeros_like(nodal_force)
    residual = nodal_force
    direction = nodal_force
    norm_gram = gram_local(residual, residual)
    for iteration in range(ITERS):
        applied = apply_operator(direction)
        curvature = gram_local(direction, applied)
        curvature = 0.5 * (curvature + curvature.T)
        step_alpha = solve_small(curvature, norm_gram)
        displacement = displacement + combine(direction, step_alpha)
        residual = residual - combine(applied, step_alpha)
        if iteration + 1 < ITERS:
            norm_next = gram_local(residual, residual)
            step_beta = solve_small(norm_gram, norm_next)
            direction = residual + combine(direction, step_beta)
            norm_gram = norm_next
    return (displacement, residual)
```

```python
import functools

import jax
import jax.numpy as jnp
import numpy as np
from jax import lax
from jax.experimental import pallas as pl
from jax.experimental.pallas import tpu as pltpu
from jax.sharding import PartitionSpec as P

LOADS = 8
ROWS = 24
SPRING = 0.5
SPLIT = 16
GROUP = 8
VMEM_LIMIT = 48 * 1024 * 1024

VMEM = pl.BlockSpec(memory_space=pltpu.VMEM)
SMEM = pl.BlockSpec(memory_space=pltpu.SMEM)
PARAMS = pltpu.CompilerParams(vmem_limit_bytes=VMEM_LIMIT)

_d, _l, _m = np.meshgrid(np.arange(8), np.arange(8), np.arange(8), indexing="ij")
DIAGONALS = ((_m - _l) % 8 == _d).astype(np.float32)


def to_diagonals(matrix):
    return jnp.sum(DIAGONALS * matrix[None], axis=1)


def from_diagonals(diagonals):
    return jnp.sum(DIAGONALS * diagonals[:, None, :], axis=0)


def spread(matrices, width):
    stacked = jnp.stack([to_diagonals(m) for m in matrices])
    return jnp.broadcast_to(stacked[..., None], stacked.shape + (width,))


def pack_kernel(capacity, owner_ref, live_ref, force_ref, voxel_ref, out_ref, count_ref):
    devices, rows, _, width = out_ref.shape
    blocks = owner_ref.shape[0]
    empty = jnp.full((8, width), -1.0, jnp.float32)
    zero = jnp.zeros((8, width), jnp.float32)

    def clear(dev, carry):
        count_ref[dev] = 0
        for row in range(rows):
            out_ref[dev, row] = zero if row < 3 * capacity else empty
        return carry

    lax.fori_loop(0, devices, clear, 0)
    lane = lax.broadcasted_iota(jnp.int32, (8, width), 1)
    sub = lax.broadcasted_iota(jnp.int32, (8, width), 0)

    def place(block, carry):
        owner = owner_ref[block]
        rank = count_ref[owner]
        count_ref[owner] = rank + 1
        limit = jnp.full((8, width), live_ref[block, 0], jnp.int32)
        for load in range(1, LOADS):
            limit = jnp.where(sub == load, live_ref[block, load], limit)
        keep = lane < limit
        for k in range(3):
            value = force_ref[block, k * 8 : k * 8 + 8, :]
            out_ref[owner, rank * 3 + k] = jnp.where(keep, value, 0.0)
        ids = voxel_ref[pl.ds(block, 1), :].astype(jnp.float32)
        out_ref[owner, 3 * capacity + rank // 8, pl.ds(rank % 8, 1), :] = ids
        return carry

    lax.fori_loop(0, blocks, place, 0)


def pack(owner, live, force, voxel, devices, capacity):
    rows = 3 * capacity + -(-capacity // 8)
    return pl.pallas_call(
        functools.partial(pack_kernel, capacity),
        out_shape=jax.ShapeDtypeStruct((devices, rows, 8, force.shape[2]), jnp.float32),
        in_specs=[SMEM, SMEM, VMEM, VMEM],
        out_specs=VMEM,
        scratch_shapes=[pltpu.SMEM((devices,), jnp.int32)],
        compiler_params=PARAMS,
    )(owner, live, force, voxel)


def scatter_kernel(capacity, width_x, valid_ref, got_ref, out_ref, left_ref, acc_ref, list_ref):
    devices, rows, _, width = got_ref.shape
    total = devices * capacity
    slots = GROUP * width
    cols = acc_ref.shape[2]
    tiles = acc_ref.shape[0]

    def gather(block, count):
        list_ref[count] = block
        return count + (valid_ref[block] > 0).astype(jnp.int32)

    count = lax.fori_loop(0, total, gather, jnp.int32(0))

    def clear(tile, carry):
        acc_ref[tile] = jnp.zeros(acc_ref.shape[1:], jnp.float32)
        return carry

    lax.fori_loop(0, tiles, clear, 0)
    column = lax.broadcasted_iota(jnp.int32, (cols, slots), 0)

    def step(index, carry):
        parts = []
        ids = []
        for j in range(GROUP):
            place = index * GROUP + j
            block = list_ref[jnp.where(place < count, place, 0)]
            dev = block // capacity
            slot = block % capacity
            parts.append(
                jnp.concatenate([got_ref[dev, slot * 3 + k] for k in range(3)], axis=0)
            )
            row = got_ref[dev, 3 * capacity + slot // 8, pl.ds(slot % 8, 1), :]
            ids.append(jnp.where(place < count, row, -1.0))
        values = jnp.concatenate(parts, axis=1)
        voxel = jnp.concatenate(ids, axis=1).astype(jnp.int32)
        high = values.astype(jnp.bfloat16).astype(jnp.float32)
        low = values - high
        both = jnp.concatenate([high, low], axis=0)
        line = lax.shift_right_arithmetic(voxel, 10)
        along = jnp.bitwise_and(voxel, tiles * cols - 1)
        for r in range(SPLIT):
            left_ref[r * 48 : r * 48 + 48, :] = jnp.where(line == r, both, 0.0).astype(
                jnp.bfloat16
            )

        def tile(t, inner):
            right = jnp.where(column == along - t * cols, 1.0, 0.0).astype(jnp.bfloat16)
            acc_ref[t] += lax.dot_general(
                left_ref[...],
                right,
                (((1,), (1,)), ((), ())),
                preferred_element_type=jnp.float32,
            )
            return inner

        lax.fori_loop(0, tiles, tile, 0)
        return carry

    lax.fori_loop(0, (count + GROUP - 1) // GROUP, step, 0)
    for r in range(SPLIT):
        for t in range(tiles):
            out_ref[r * tiles + t] = (
                acc_ref[t, r * 48 : r * 48 + 24, :] + acc_ref[t, r * 48 + 24 : r * 48 + 48, :]
            )


def scatter(got, capacity, depth, height, width_x):
    volume = depth * height * width_x
    tiles = volume // SPLIT // width_x
    assert volume // SPLIT == 1024
    first = got[:, 3 * capacity :, :, 0].reshape(got.shape[0], -1)[:, :capacity]
    valid = (first >= 0.0).astype(jnp.int32).reshape(-1)
    return pl.pallas_call(
        functools.partial(scatter_kernel, capacity, width_x),
        out_shape=jax.ShapeDtypeStruct((depth * height, ROWS, width_x), jnp.float32),
        in_specs=[SMEM, VMEM],
        out_specs=VMEM,
        scratch_shapes=[
            pltpu.VMEM((SPLIT * 48, GROUP * got.shape[3]), jnp.bfloat16),
            pltpu.VMEM((tiles, SPLIT * 48, width_x), jnp.float32),
            pltpu.SMEM((valid.shape[0] + 1,), jnp.int32),
        ],
        compiler_params=PARAMS,
    )(valid, got)


def shift_left(value):
    width = value.shape[-1]
    lane = lax.broadcasted_iota(jnp.int32, value.shape, 1)
    return jnp.where(lane == width - 1, 0.0, pltpu.roll(value, width - 1, 1))


def shift_right(value):
    lane = lax.broadcasted_iota(jnp.int32, value.shape, 1)
    return jnp.where(lane == 0, 0.0, pltpu.roll(value, 1, 1))


def mixed(value, coefficients):
    parts = []
    for k in range(3):
        piece = value[k * 8 : k * 8 + 8]
        total = piece * coefficients[0]
        for s in range(1, 8):
            total = total + pltpu.roll(piece, s, 0) * coefficients[s]
        parts.append(total)
    return jnp.concatenate(parts, axis=0)


def store_split(split_ref, z, y, value):
    both = jnp.concatenate([value, shift_left(value)], axis=0)
    high = both.astype(jnp.bfloat16)
    low = (both - high.astype(jnp.float32)).astype(jnp.bfloat16)
    split_ref[z, y, 0:48, :] = high
    split_ref[z, y, 48:96, :] = low


def run_operator(split_ref, field, weight_ref, weight_at, matrix_ref, out_ref, carry_ref):
    planes, lines = split_ref.shape[0] - 1, split_ref.shape[1] - 1
    matrix = matrix_ref[...]

    def plane(ze, carry):
        weights = weight_ref[ze + weight_at]
        before = None
        for ye in range(lines):
            corners = [split_ref.at[ze + a, ye + b] for a in (0, 1) for b in (0, 1)]
            high = jnp.concatenate([c[0:48, :] for c in corners], axis=0)
            low = jnp.concatenate([c[48:96, :] for c in corners], axis=0)
            forces = jnp.dot(
                matrix,
                jnp.concatenate([high, high, low], axis=0),
                preferred_element_type=jnp.float32,
            )
            forces = forces * weights[ye + weight_at : ye + weight_at + 1, :]
            if ye > 0:
                n = ye - 1
                lower = forces[0:48] + before[48:96] + carry_ref[n]
                carry_ref[n] = forces[96:144] + before[144:192]
                result = lower[0:24] + shift_right(lower[24:48])
                out_ref[ze, n] = result + SPRING * field(ze, ye)
            before = forces
        return carry

    carry_ref[...] = jnp.zeros(carry_ref.shape, jnp.float32)
    lax.fori_loop(0, planes, plane, 0)


def run_grams(first, second, depth, height, gram_ref):
    width = gram_ref.shape[-1]

    def plane(z, carry):
        sums = list(carry)
        for y in range(height):
            a = first(z, y)
            b = second(z, y)
            for k in range(3):
                a8 = a[k * 8 : k * 8 + 8]
                b8 = b[k * 8 : k * 8 + 8]
                for s in range(8):
                    rolled = a8 if s == 0 else pltpu.roll(a8, s, 0)
                    for h in range(0, a8.shape[1], width):
                        sums[s] = sums[s] + rolled[:, h : h + width] * a8[:, h : h + width]
                        sums[8 + s] = sums[8 + s] + rolled[:, h : h + width] * b8[:, h : h + width]
        return tuple(sums)

    sums = lax.fori_loop(0, depth, plane, tuple(jnp.zeros((8, width), jnp.float32) for _ in range(16)))
    for s in range(16):
        gram_ref[s // 8, s % 8] = sums[s]


def first_kernel(field_ref, weight_ref, matrix_ref, out_ref, gram_ref, split_ref, carry_ref):
    depth, lines = field_ref.shape[0], field_ref.shape[1]

    def split(z, carry):
        for y in range(lines):
            store_split(split_ref, z, y, field_ref[z, y])
        return carry

    lax.fori_loop(0, depth, split, 0)
    run_operator(
        split_ref, lambda z, y: field_ref[z, y], weight_ref, 0, matrix_ref, out_ref, carry_ref
    )
    run_grams(
        lambda z, y: field_ref[z + 2, y + 2],
        lambda z, y: out_ref[z + 2, y + 1],
        depth - 4,
        lines - 4,
        gram_ref,
    )


def second_kernel(
    inside_ref, coef_ref, field_ref, applied_ref, weight_ref, matrix_ref,
    res_ref, out_ref, gram_ref, split_ref, carry_ref, full_ref,
):
    depth, lines = full_ref.shape[0], full_ref.shape[1]

    def split(z, carry):
        coef = [coef_ref[0, s] for s in range(8)]
        for y in range(lines):
            value = field_ref[z + 1, y + 1] - mixed(applied_ref[z + 1, y], coef)
            value = value * inside_ref[z, y]
            full_ref[z, y] = value
            store_split(split_ref, z, y, value)
        return carry

    lax.fori_loop(0, depth, split, 0)
    run_operator(
        split_ref, lambda z, y: full_ref[z, y], weight_ref, 1, matrix_ref, out_ref, carry_ref
    )
    run_grams(
        lambda z, y: full_ref[z + 1, y + 1],
        lambda z, y: out_ref[z + 1, y],
        depth - 2,
        lines - 2,
        gram_ref,
    )

    def keep(z, carry):
        for y in range(lines - 2):
            res_ref[z, y] = full_ref[z + 1, y + 1]
        return carry

    lax.fori_loop(0, depth - 2, keep, 0)


def last_kernel(coef_ref, field_ref, res_ref, first_ref, second_ref, disp_ref, out_ref):
    depth, lines = res_ref.shape[0], res_ref.shape[1]

    def plane(z, carry):
        coefs = [[coef_ref[i, s] for s in range(8)] for i in range(3)]
        for y in range(lines):
            residual = res_ref[z, y]
            disp = mixed(field_ref[z + 2, y + 2], coefs[0]) + mixed(residual, coefs[1])
            left = residual - mixed(second_ref[z + 1, y], coefs[1])
            left = left - mixed(first_ref[z + 2, y + 1], coefs[2])
            disp_ref[:, z, y, :] = disp
            out_ref[:, z, y, :] = left
        return carry

    lax.fori_loop(0, depth, plane, 0)


def first_operator(field, weights, matrix):
    depth, lines, _, width = field.shape
    return pl.pallas_call(
        first_kernel,
        out_shape=(
            jax.ShapeDtypeStruct((depth - 1, lines - 2, ROWS, width), jnp.float32),
            jax.ShapeDtypeStruct((2, 8, 8, 128), jnp.float32),
        ),
        in_specs=[VMEM] * 3,
        out_specs=(VMEM, VMEM),
        scratch_shapes=[
            pltpu.VMEM((depth, lines, 96, width), jnp.bfloat16),
            pltpu.VMEM((lines - 2, 48, width), jnp.float32),
        ],
        compiler_params=PARAMS,
    )(field, weights, matrix)


def second_operator(inside, coef, field, applied, weights, matrix):
    depth, lines, _, width = field.shape
    depth, lines = depth - 2, lines - 2
    return pl.pallas_call(
        second_kernel,
        out_shape=(
            jax.ShapeDtypeStruct((depth - 2, lines - 2, ROWS, width), jnp.float32),
            jax.ShapeDtypeStruct((depth - 1, lines - 2, ROWS, width), jnp.float32),
            jax.ShapeDtypeStruct((2, 8, 8, 128), jnp.float32),
        ),
        in_specs=[SMEM] + [VMEM] * 5,
        out_specs=(VMEM, VMEM, VMEM),
        scratch_shapes=[
            pltpu.VMEM((depth, lines, 96, width), jnp.bfloat16),
            pltpu.VMEM((lines - 2, 48, width), jnp.float32),
            pltpu.VMEM((depth, lines, ROWS, width), jnp.float32),
        ],
        compiler_params=PARAMS,
    )(inside, coef, field, applied, weights, matrix)


def last_update(coef, field, residual, first, second):
    depth, lines, _, width = residual.shape
    shape = jax.ShapeDtypeStruct((ROWS, depth, lines, width), jnp.float32)
    return pl.pallas_call(
        last_kernel,
        out_shape=(shape, shape),
        in_specs=[VMEM] * 5,
        out_specs=(VMEM, VMEM),
        compiler_params=PARAMS,
    )(coef, field, residual, first, second)


def with_halo(block, axis, dim, below, above):
    count = lax.axis_size(axis)
    forward = [(i, i + 1) for i in range(count - 1)]
    backward = [(target, source) for source, target in forward]
    size = block.shape[dim]
    low = lax.ppermute(lax.slice_in_dim(block, size - below, None, axis=dim), axis, forward)
    high = lax.ppermute(lax.slice_in_dim(block, 0, above, axis=dim), axis, backward)
    return jnp.concatenate([low, block, high], axis=dim)


def solve_small(matrix, target):
    factor = jnp.linalg.cholesky(matrix)
    halfway = lax.linalg.triangular_solve(factor, target, left_side=True, lower=True)
    return lax.linalg.triangular_solve(
        factor, halfway, left_side=True, lower=True, transpose_a=True
    )


def total_grams(gram):
    sums = lax.psum(jnp.sum(gram, axis=-1), ("gz", "gy"))
    return from_diagonals(sums[0]), from_diagonals(sums[1])


def small_dot(a, b):
    return jnp.sum(a[:, :, None] * b[None, :, :], axis=1)


def body(patch_force, patch_owner, patch_voxel, patch_live, voxel_mask, element_matrix):
    depth, height, width = voxel_mask.shape
    groups_z = lax.axis_size("gz")
    groups_y = lax.axis_size("gy")
    devices = groups_z * groups_y
    blocks = patch_force.shape[0]
    capacity = max(2, (2 * blocks + devices - 1) // devices)

    packed = pack(patch_owner, patch_live, patch_force, patch_voxel, devices, capacity)
    got = lax.all_to_all(
        packed.reshape(devices, -1, packed.shape[3]), ("gz", "gy"), split_axis=0, concat_axis=0, tiled=True
    ).reshape(packed.shape)

    weights = with_halo(voxel_mask, "gz", 0, 2, 1)
    weights = with_halo(weights, "gy", 1, 2, 1).astype(jnp.float32)
    wide = jnp.kron(element_matrix, jnp.eye(LOADS, dtype=jnp.float32))
    high = wide.astype(jnp.bfloat16)
    low = (wide - lax.reduce_precision(wide, 8, 7)).astype(jnp.bfloat16)
    matrix = jnp.concatenate([high, low, high], axis=1)
    node_z = jnp.arange(depth + 2) - 1 + lax.axis_index("gz") * depth
    node_y = jnp.arange(height + 2) - 1 + lax.axis_index("gy") * height
    inside_z = (node_z >= 0) & (node_z < groups_z * depth)
    inside_y = (node_y >= 0) & (node_y < groups_y * height)
    inside = (inside_z[:, None] & inside_y[None, :]).astype(jnp.float32)

    force = scatter(got, capacity, depth, height, width).reshape(depth, height, ROWS, width)
    field = with_halo(force, "gz", 0, 2, 2)
    field = with_halo(field, "gy", 1, 2, 2)

    applied, gram = first_operator(field, weights, matrix)
    norm_gram, curvature = total_grams(gram)
    curvature = 0.5 * (curvature + curvature.T)
    alpha = solve_small(curvature, norm_gram)

    residual, again, gram = second_operator(
        inside, spread([alpha], width), field, applied, weights, matrix
    )
    norm_next, cross = total_grams(gram)
    beta = solve_small(norm_gram, norm_next)
    curvature = cross - small_dot(small_dot(beta.T, curvature), beta)
    curvature = 0.5 * (curvature + curvature.T)
    alpha_next = solve_small(curvature, norm_next)
    joint = small_dot(beta, alpha_next)

    coef = spread([alpha + joint, alpha_next, joint], width)
    return last_update(coef, field, residual, applied, again)


def solution(mesh):
    placed = (
        P(("gz", "gy"), None, None),
        P(("gz", "gy")),
        P(("gz", "gy"), None),
        P(("gz", "gy"), None),
        P("gz", "gy", None),
        P(),
    )
    return jax.shard_map(
        body,
        mesh=mesh,
        in_specs=placed,
        out_specs=(P(None, "gz", "gy", None), P(None, "gz", "gy", None)),
        check_vma=False,
    )
```

```python
import functools

import jax
import jax.numpy as jnp
import numpy as np
from jax import lax
from jax.experimental import pallas as pl
from jax.experimental.pallas import tpu as pltpu
from jax.sharding import PartitionSpec as P

LOADS = 8
ROWS = 24
SPRING = 0.5
SPLIT = 16
GROUP = 8
VMEM_LIMIT = 48 * 1024 * 1024

VMEM = pl.BlockSpec(memory_space=pltpu.VMEM)
SMEM = pl.BlockSpec(memory_space=pltpu.SMEM)
PARAMS = pltpu.CompilerParams(vmem_limit_bytes=VMEM_LIMIT)

_d, _l, _m = np.meshgrid(np.arange(8), np.arange(8), np.arange(8), indexing="ij")
DIAGONALS = ((_m - _l) % 8 == _d).astype(np.float32)


def to_diagonals(matrix):
    return jnp.sum(DIAGONALS * matrix[None], axis=1)


def from_diagonals(diagonals):
    return jnp.sum(DIAGONALS * diagonals[:, None, :], axis=0)


def spread(matrices, width):
    stacked = jnp.stack([to_diagonals(m) for m in matrices])
    return jnp.broadcast_to(stacked[..., None], stacked.shape + (width,))


def pack_kernel(shares, owner_ref, live_ref, force_ref, voxel_ref, near_ref, far_ref, count_ref):
    blocks = owner_ref.shape[0]
    devices, _, _, width = near_ref.shape
    empty = jnp.full((8, width), -1.0, jnp.float32)
    zero = jnp.zeros((8, width), jnp.float32)

    def clear(dev, carry):
        count_ref[dev] = 0
        for out_ref, share in zip((near_ref, far_ref), shares):
            for row in range(out_ref.shape[1]):
                out_ref[dev, row] = zero if row < 3 * share else empty
        return carry

    lax.fori_loop(0, devices, clear, 0)
    lane = lax.broadcasted_iota(jnp.int32, (8, width), 1)
    sub = lax.broadcasted_iota(jnp.int32, (8, width), 0)

    def place(block, carry):
        owner = owner_ref[block]
        rank = count_ref[owner]
        count_ref[owner] = rank + 1
        limit = jnp.full((8, width), live_ref[block, 0], jnp.int32)
        for load in range(1, LOADS):
            limit = jnp.where(sub == load, live_ref[block, load], limit)
        keep = lane < limit
        values = [
            jnp.where(keep, force_ref[block, k * 8 : k * 8 + 8, :], 0.0) for k in range(3)
        ]
        ids = voxel_ref[pl.ds(block, 1), :].astype(jnp.float32)

        def store(out_ref, share, slot):
            for k in range(3):
                out_ref[owner, slot * 3 + k] = values[k]
            out_ref[owner, 3 * share + slot // 8, pl.ds(slot % 8, 1), :] = ids

        @pl.when(rank < shares[0])
        def _():
            store(near_ref, shares[0], rank)

        @pl.when(rank >= shares[0])
        def _():
            store(far_ref, shares[1], rank - shares[0])

        return carry

    lax.fori_loop(0, blocks, place, 0)


def pack(owner, live, force, voxel, devices, shares):
    return pl.pallas_call(
        functools.partial(pack_kernel, shares),
        out_shape=tuple(
            jax.ShapeDtypeStruct((devices, 3 * c + -(-c // 8), 8, force.shape[2]), jnp.float32)
            for c in shares
        ),
        in_specs=[SMEM, SMEM, VMEM, VMEM],
        out_specs=(VMEM, VMEM),
        scratch_shapes=[pltpu.SMEM((devices,), jnp.int32)],
        compiler_params=PARAMS,
    )(owner, live, force, voxel)


def scatter_kernel(capacity, valid_ref, got_ref, *refs):
    before_ref = refs[0] if len(refs) == 5 else None
    out_ref, left_ref, acc_ref, list_ref = refs[-4:]
    devices, rows, _, width = got_ref.shape
    total = devices * capacity
    slots = GROUP * width
    cols = acc_ref.shape[2]
    tiles = acc_ref.shape[0]

    def gather(block, count):
        list_ref[count] = block
        return count + (valid_ref[block] > 0).astype(jnp.int32)

    count = lax.fori_loop(0, total, gather, jnp.int32(0))

    def clear(tile, carry):
        acc_ref[tile] = jnp.zeros(acc_ref.shape[1:], jnp.float32)
        return carry

    lax.fori_loop(0, tiles, clear, 0)
    column = lax.broadcasted_iota(jnp.int32, (cols, slots), 0)

    def step(index, carry):
        parts = []
        ids = []
        for j in range(GROUP):
            place = index * GROUP + j
            block = list_ref[jnp.where(place < count, place, 0)]
            dev = block // capacity
            slot = block % capacity
            parts.append(
                jnp.concatenate([got_ref[dev, slot * 3 + k] for k in range(3)], axis=0)
            )
            row = got_ref[dev, 3 * capacity + slot // 8, pl.ds(slot % 8, 1), :]
            ids.append(jnp.where(place < count, row, -1.0))
        values = jnp.concatenate(parts, axis=1)
        voxel = jnp.concatenate(ids, axis=1).astype(jnp.int32)
        high = values.astype(jnp.bfloat16).astype(jnp.float32)
        low = values - high
        both = jnp.concatenate([high, low], axis=0)
        line = lax.shift_right_arithmetic(voxel, 10)
        along = jnp.bitwise_and(voxel, tiles * cols - 1)
        for r in range(SPLIT):
            left_ref[r * 48 : r * 48 + 48, :] = jnp.where(line == r, both, 0.0).astype(
                jnp.bfloat16
            )

        def tile(t, inner):
            right = jnp.where(column == along - t * cols, 1.0, 0.0).astype(jnp.bfloat16)
            acc_ref[t] += lax.dot_general(
                left_ref[...],
                right,
                (((1,), (1,)), ((), ())),
                preferred_element_type=jnp.float32,
            )
            return inner

        lax.fori_loop(0, tiles, tile, 0)
        return carry

    lax.fori_loop(0, (count + GROUP - 1) // GROUP, step, 0)
    for r in range(SPLIT):
        for t in range(tiles):
            high = acc_ref[t, r * 48 : r * 48 + 24, :]
            result = high + acc_ref[t, r * 48 + 24 : r * 48 + 48, :]
            if before_ref is not None:
                result = result + before_ref[r * tiles + t]
            out_ref[r * tiles + t] = result


def scatter(got, capacity, depth, height, width_x, before=None):
    volume = depth * height * width_x
    tiles = volume // SPLIT // width_x
    assert volume // SPLIT == 1024
    first = got[:, 3 * capacity :, :, 0].reshape(got.shape[0], -1)[:, :capacity]
    valid = (first >= 0.0).astype(jnp.int32).reshape(-1)
    arrays = (valid, got) if before is None else (valid, got, before)
    slots = got.shape[0] * capacity * got.shape[3]
    return pl.pallas_call(
        functools.partial(scatter_kernel, capacity),
        out_shape=jax.ShapeDtypeStruct((depth * height, ROWS, width_x), jnp.float32),
        in_specs=[SMEM] + [VMEM] * (len(arrays) - 1),
        out_specs=VMEM,
        cost_estimate=pl.CostEstimate(
            flops=4 * SPLIT * 48 * 1024 * slots, bytes_accessed=4 * got.size, transcendentals=0
        ),
        scratch_shapes=[
            pltpu.VMEM((SPLIT * 48, GROUP * got.shape[3]), jnp.bfloat16),
            pltpu.VMEM((tiles, SPLIT * 48, width_x), jnp.float32),
            pltpu.SMEM((valid.shape[0] + 1,), jnp.int32),
        ],
        compiler_params=PARAMS,
    )(*arrays)


def shift_left(value):
    width = value.shape[-1]
    lane = lax.broadcasted_iota(jnp.int32, value.shape, 1)
    return jnp.where(lane == width - 1, 0.0, pltpu.roll(value, width - 1, 1))


def shift_right(value):
    lane = lax.broadcasted_iota(jnp.int32, value.shape, 1)
    return jnp.where(lane == 0, 0.0, pltpu.roll(value, 1, 1))


def mixed(value, coefficients):
    parts = []
    for k in range(3):
        piece = value[k * 8 : k * 8 + 8]
        total = piece * coefficients[0]
        for s in range(1, 8):
            total = total + pltpu.roll(piece, s, 0) * coefficients[s]
        parts.append(total)
    return jnp.concatenate(parts, axis=0)


def store_split(split_ref, z, y, value):
    both = jnp.concatenate([value, shift_left(value)], axis=0)
    high = both.astype(jnp.bfloat16)
    low = (both - high.astype(jnp.float32)).astype(jnp.bfloat16)
    split_ref[z, y, 0:48, :] = high
    split_ref[z, y, 48:96, :] = low


def run_operator(split_ref, field, weight_ref, weight_at, matrix_ref, out_ref, carry_ref):
    planes, lines = split_ref.shape[0] - 1, split_ref.shape[1] - 1
    matrix = matrix_ref[...]

    def plane(ze, carry):
        weights = weight_ref[ze + weight_at]
        before = None
        for ye in range(lines):
            corners = [split_ref.at[ze + a, ye + b] for a in (0, 1) for b in (0, 1)]
            high = jnp.concatenate([c[0:48, :] for c in corners], axis=0)
            low = jnp.concatenate([c[48:96, :] for c in corners], axis=0)
            forces = jnp.dot(
                matrix,
                jnp.concatenate([high, high, low], axis=0),
                preferred_element_type=jnp.float32,
            )
            forces = forces * weights[ye + weight_at : ye + weight_at + 1, :]
            if ye > 0:
                n = ye - 1
                lower = forces[0:48] + before[48:96] + carry_ref[n]
                carry_ref[n] = forces[96:144] + before[144:192]
                result = lower[0:24] + shift_right(lower[24:48])
                out_ref[ze, n] = result + SPRING * field(ze, ye)
            before = forces
        return carry

    carry_ref[...] = jnp.zeros(carry_ref.shape, jnp.float32)
    lax.fori_loop(0, planes, plane, 0)


def run_grams(first, second, depth, height, gram_ref):
    width = gram_ref.shape[1]

    def plane(z, carry):
        sums = list(carry)
        for y in range(height):
            a = first(z, y)
            b = second(z, y)
            for k in range(3):
                a8 = a[k * 8 : k * 8 + 8]
                b8 = b[k * 8 : k * 8 + 8]
                for s in range(8):
                    rolled = a8 if s == 0 else pltpu.roll(a8, s, 0)
                    for h in range(0, a8.shape[1], width):
                        sums[s] = sums[s] + rolled[:, h : h + width] * a8[:, h : h + width]
                        sums[8 + s] = sums[8 + s] + rolled[:, h : h + width] * b8[:, h : h + width]
        return tuple(sums)

    sums = lax.fori_loop(0, depth, plane, tuple(jnp.zeros((8, width), jnp.float32) for _ in range(16)))
    lane = lax.broadcasted_iota(jnp.int32, (8, width), 1)
    tile = jnp.zeros((8, width), jnp.float32)
    for s in range(16):
        tile = jnp.where(lane == s, jnp.sum(sums[s], axis=1, keepdims=True), tile)
    gram_ref[...] = tile


def first_kernel(field_ref, weight_ref, matrix_ref, out_ref, gram_ref, split_ref, carry_ref):
    depth, lines = field_ref.shape[0], field_ref.shape[1]

    def split(z, carry):
        for y in range(lines):
            store_split(split_ref, z, y, field_ref[z, y])
        return carry

    lax.fori_loop(0, depth, split, 0)
    run_operator(
        split_ref, lambda z, y: field_ref[z, y], weight_ref, 0, matrix_ref, out_ref, carry_ref
    )
    run_grams(
        lambda z, y: field_ref[z + 2, y + 2],
        lambda z, y: out_ref[z + 2, y + 1],
        depth - 4,
        lines - 4,
        gram_ref,
    )


def second_kernel(
    inside_ref, coef_ref, field_ref, applied_ref, weight_ref, matrix_ref,
    res_ref, out_ref, gram_ref, split_ref, carry_ref, full_ref,
):
    depth, lines = full_ref.shape[0], full_ref.shape[1]

    def split(z, carry):
        coef = [coef_ref[0, s] for s in range(8)]
        for y in range(lines):
            value = field_ref[z + 1, y + 1] - mixed(applied_ref[z + 1, y], coef)
            value = value * inside_ref[z, y]
            full_ref[z, y] = value
            store_split(split_ref, z, y, value)
        return carry

    lax.fori_loop(0, depth, split, 0)
    run_operator(
        split_ref, lambda z, y: full_ref[z, y], weight_ref, 1, matrix_ref, out_ref, carry_ref
    )
    run_grams(
        lambda z, y: full_ref[z + 1, y + 1],
        lambda z, y: out_ref[z + 1, y],
        depth - 2,
        lines - 2,
        gram_ref,
    )

    def keep(z, carry):
        for y in range(lines - 2):
            res_ref[z, y] = full_ref[z + 1, y + 1]
        return carry

    lax.fori_loop(0, depth - 2, keep, 0)


def last_kernel(coef_ref, field_ref, res_ref, first_ref, second_ref, disp_ref, out_ref):
    depth, lines = res_ref.shape[0], res_ref.shape[1]

    def plane(z, carry):
        coefs = [[coef_ref[i, s] for s in range(8)] for i in range(3)]
        for y in range(lines):
            residual = res_ref[z, y]
            disp = mixed(field_ref[z + 2, y + 2], coefs[0]) + mixed(residual, coefs[1])
            left = residual - mixed(second_ref[z + 1, y], coefs[1])
            left = left - mixed(first_ref[z + 2, y + 1], coefs[2])
            disp_ref[:, z, y, :] = disp
            out_ref[:, z, y, :] = left
        return carry

    lax.fori_loop(0, depth, plane, 0)


def first_operator(field, weights, matrix):
    depth, lines, _, width = field.shape
    return pl.pallas_call(
        first_kernel,
        out_shape=(
            jax.ShapeDtypeStruct((depth - 1, lines - 2, ROWS, width), jnp.float32),
            jax.ShapeDtypeStruct((8, 128), jnp.float32),
        ),
        in_specs=[VMEM] * 3,
        out_specs=(VMEM, VMEM),
        scratch_shapes=[
            pltpu.VMEM((depth, lines, 96, width), jnp.bfloat16),
            pltpu.VMEM((lines - 2, 48, width), jnp.float32),
        ],
        compiler_params=PARAMS,
    )(field, weights, matrix)


def second_operator(inside, coef, field, applied, weights, matrix):
    depth, lines, _, width = field.shape
    depth, lines = depth - 2, lines - 2
    return pl.pallas_call(
        second_kernel,
        out_shape=(
            jax.ShapeDtypeStruct((depth - 2, lines - 2, ROWS, width), jnp.float32),
            jax.ShapeDtypeStruct((depth - 1, lines - 2, ROWS, width), jnp.float32),
            jax.ShapeDtypeStruct((8, 128), jnp.float32),
        ),
        in_specs=[SMEM] + [VMEM] * 5,
        out_specs=(VMEM, VMEM, VMEM),
        scratch_shapes=[
            pltpu.VMEM((depth, lines, 96, width), jnp.bfloat16),
            pltpu.VMEM((lines - 2, 48, width), jnp.float32),
            pltpu.VMEM((depth, lines, ROWS, width), jnp.float32),
        ],
        compiler_params=PARAMS,
    )(inside, coef, field, applied, weights, matrix)


def last_update(coef, field, residual, first, second):
    depth, lines, _, width = residual.shape
    shape = jax.ShapeDtypeStruct((ROWS, depth, lines, width), jnp.float32)
    return pl.pallas_call(
        last_kernel,
        out_shape=(shape, shape),
        in_specs=[VMEM] * 5,
        out_specs=(VMEM, VMEM),
        compiler_params=PARAMS,
    )(coef, field, residual, first, second)


def with_halo(block, axis, dim, below, above):
    count = lax.axis_size(axis)
    forward = [(i, i + 1) for i in range(count - 1)]
    backward = [(target, source) for source, target in forward]
    size = block.shape[dim]
    low = lax.ppermute(lax.slice_in_dim(block, size - below, None, axis=dim), axis, forward)
    high = lax.ppermute(lax.slice_in_dim(block, 0, above, axis=dim), axis, backward)
    return jnp.concatenate([low, block, high], axis=dim)


def solve_small(matrix, target):
    factor = jnp.linalg.cholesky(matrix)
    halfway = lax.linalg.triangular_solve(factor, target, left_side=True, lower=True)
    return lax.linalg.triangular_solve(
        factor, halfway, left_side=True, lower=True, transpose_a=True
    )


def reduce_kernel(counts, tile_ref, out_ref, line_ref, plane_ref, mid_ref, send_sems, recv_sems):
    nz, ny = counts
    gz, gy = lax.axis_index("gz"), lax.axis_index("gy")
    beside = [(gz, lax.rem(gy + d, ny)) for d in range(1, ny)]
    along = [(lax.rem(gz + d, nz), gy) for d in range(1, nz)]
    barrier = pltpu.get_barrier_semaphore()
    for peer in beside + along:
        pl.semaphore_signal(barrier, inc=1, device_id=peer, device_id_type=pl.DeviceIdType.MESH)
    pl.semaphore_wait(barrier, ny + nz - 2)

    def exchange(source_ref, slots_ref, place, peers, first):
        copies = [
            pltpu.make_async_remote_copy(
                src_ref=source_ref,
                dst_ref=slots_ref.at[place],
                send_sem=send_sems.at[first + i],
                recv_sem=recv_sems.at[first + i],
                device_id=peer,
                device_id_type=pl.DeviceIdType.MESH,
            )
            for i, peer in enumerate(peers)
        ]
        for copy in copies:
            copy.start()
        slots_ref[place] = source_ref[...]
        for copy in copies:
            copy.wait()
        total = slots_ref[0]
        for i in range(1, slots_ref.shape[0]):
            total = total + slots_ref[i]
        return total

    mid_ref[...] = exchange(tile_ref, line_ref, gy, beside, 0)
    out_ref[...] = exchange(mid_ref, plane_ref, gz, along, ny - 1)


def total_grams(tile):
    nz, ny = lax.axis_size("gz"), lax.axis_size("gy")
    sums = pl.pallas_call(
        functools.partial(reduce_kernel, (nz, ny)),
        out_shape=jax.ShapeDtypeStruct(tile.shape, jnp.float32),
        in_specs=[VMEM],
        out_specs=VMEM,
        scratch_shapes=[
            pltpu.VMEM((ny,) + tile.shape, jnp.float32),
            pltpu.VMEM((nz,) + tile.shape, jnp.float32),
            pltpu.VMEM(tile.shape, jnp.float32),
            pltpu.SemaphoreType.DMA((ny + nz - 2,)),
            pltpu.SemaphoreType.DMA((ny + nz - 2,)),
        ],
        compiler_params=pltpu.CompilerParams(collective_id=0, has_side_effects=True),
    )(tile)
    sums = sums[:, :16].T
    return from_diagonals(sums[:8]), from_diagonals(sums[8:])


def halo_kernel(counts, halo, field_ref, out_ref, send_sems, recv_sems):
    nz, ny = counts
    depth, lines = field_ref.shape[:2]
    gz, gy = lax.axis_index("gz"), lax.axis_index("gy")
    ways = [(dz, dy) for dz in (-1, 0, 1) for dy in (-1, 0, 1) if (dz, dy) != (0, 0)]

    def exists(dz, dy):
        z, y = gz + dz, gy + dy
        return (z >= 0) & (z < nz) & (y >= 0) & (y < ny)

    def source(step, size):
        return {-1: pl.ds(0, halo), 0: pl.ds(0, size), 1: pl.ds(size - halo, halo)}[step]

    def target(step, size):
        return {-1: pl.ds(halo + size, halo), 0: pl.ds(halo, size), 1: pl.ds(0, halo)}[step]

    def copy(i, sign):
        dz, dy = ways[i]
        return pltpu.make_async_remote_copy(
            src_ref=field_ref.at[source(dz, depth), source(dy, lines)],
            dst_ref=out_ref.at[target(dz, depth), target(dy, lines)],
            send_sem=send_sems.at[i],
            recv_sem=recv_sems.at[i],
            device_id=(gz + sign * dz, gy + sign * dy),
            device_id_type=pl.DeviceIdType.MESH,
        )

    barrier = pltpu.get_barrier_semaphore()
    peers = jnp.int32(0)
    for dz, dy in ways:
        peers = peers + jnp.where(exists(dz, dy), 1, 0)

        @pl.when(exists(dz, dy))
        def _():
            pl.semaphore_signal(
                barrier, inc=1, device_id=(gz + dz, gy + dy), device_id_type=pl.DeviceIdType.MESH
            )

    pl.semaphore_wait(barrier, peers)
    for i, (dz, dy) in enumerate(ways):

        @pl.when(exists(dz, dy))
        def _():
            copy(i, 1).start()

    def keep(z, carry):
        for y in range(lines):
            out_ref[z + halo, y + halo] = field_ref[z, y]
        return carry

    lax.fori_loop(0, depth, keep, 0)
    for dz, dy in ways:

        @pl.when(jnp.logical_not(exists(-dz, -dy)))
        def _():
            zs, ys = target(dz, depth), target(dy, lines)

            def clear(z, carry):
                for y in range(ys.size):
                    out_ref[zs.start + z, ys.start + y] = jnp.zeros(out_ref.shape[2:], jnp.float32)
                return carry

            lax.fori_loop(0, zs.size, clear, 0)

    for i, (dz, dy) in enumerate(ways):

        @pl.when(exists(dz, dy))
        def _():
            copy(i, 1).wait_send()

        @pl.when(exists(-dz, -dy))
        def _():
            copy(i, -1).wait_recv()


def field_with_halo(field, halo):
    depth, lines, rows, width = field.shape
    counts = (lax.axis_size("gz"), lax.axis_size("gy"))
    return pl.pallas_call(
        functools.partial(halo_kernel, counts, halo),
        out_shape=jax.ShapeDtypeStruct(
            (depth + 2 * halo, lines + 2 * halo, rows, width), jnp.float32
        ),
        in_specs=[VMEM],
        out_specs=VMEM,
        scratch_shapes=[pltpu.SemaphoreType.DMA((8,)), pltpu.SemaphoreType.DMA((8,))],
        compiler_params=pltpu.CompilerParams(
            collective_id=1, has_side_effects=True, vmem_limit_bytes=VMEM_LIMIT
        ),
    )(field)


def send_packed(packed):
    flat = packed.reshape(packed.shape[0], -1, packed.shape[3])
    got = lax.all_to_all(flat, ("gz", "gy"), split_axis=0, concat_axis=0, tiled=True)
    return got.reshape(packed.shape)


def small_dot(a, b):
    return jnp.sum(a[:, :, None] * b[None, :, :], axis=1)


def body(patch_force, patch_owner, patch_voxel, patch_live, voxel_mask, element_matrix):
    depth, height, width = voxel_mask.shape
    groups_z = lax.axis_size("gz")
    groups_y = lax.axis_size("gy")
    devices = groups_z * groups_y
    blocks = patch_force.shape[0]
    capacity = max(2, (2 * blocks + devices - 1) // devices)

    shares = (capacity // 2, capacity - capacity // 2)
    near, far = pack(patch_owner, patch_live, patch_force, patch_voxel, devices, shares)
    near = send_packed(near)
    near, far = lax.optimization_barrier((near, far))
    far = send_packed(far)

    weights = with_halo(voxel_mask, "gz", 0, 2, 1)
    weights = with_halo(weights, "gy", 1, 2, 1).astype(jnp.float32)
    wide = jnp.kron(element_matrix, jnp.eye(LOADS, dtype=jnp.float32))
    high = wide.astype(jnp.bfloat16)
    low = (wide - lax.reduce_precision(wide, 8, 7)).astype(jnp.bfloat16)
    matrix = jnp.concatenate([high, low, high], axis=1)
    node_z = jnp.arange(depth + 2) - 1 + lax.axis_index("gz") * depth
    node_y = jnp.arange(height + 2) - 1 + lax.axis_index("gy") * height
    inside_z = (node_z >= 0) & (node_z < groups_z * depth)
    inside_y = (node_y >= 0) & (node_y < groups_y * height)
    inside = (inside_z[:, None] & inside_y[None, :]).astype(jnp.float32)

    force = scatter(near, shares[0], depth, height, width)
    force = scatter(far, shares[1], depth, height, width, force)
    field = field_with_halo(force.reshape(depth, height, ROWS, width), 2)

    applied, gram = first_operator(field, weights, matrix)
    norm_gram, curvature = total_grams(gram)
    curvature = 0.5 * (curvature + curvature.T)
    alpha = solve_small(curvature, norm_gram)

    residual, again, gram = second_operator(
        inside, spread([alpha], width), field, applied, weights, matrix
    )
    norm_next, cross = total_grams(gram)
    beta = solve_small(norm_gram, norm_next)
    curvature = cross - small_dot(small_dot(beta.T, curvature), beta)
    curvature = 0.5 * (curvature + curvature.T)
    alpha_next = solve_small(curvature, norm_next)
    joint = small_dot(beta, alpha_next)

    coef = spread([alpha + joint, alpha_next, joint], width)
    return last_update(coef, field, residual, applied, again)


def solution(mesh):
    placed = (
        P(("gz", "gy"), None, None),
        P(("gz", "gy")),
        P(("gz", "gy"), None),
        P(("gz", "gy"), None),
        P("gz", "gy", None),
        P(),
    )
    return jax.shard_map(
        body,
        mesh=mesh,
        in_specs=placed,
        out_specs=(P(None, "gz", "gy", None), P(None, "gz", "gy", None)),
        check_vma=False,
    )
```

```python
import functools

import jax
import jax.numpy as jnp
import numpy as np
from jax import lax
from jax.experimental import pallas as pl
from jax.experimental.pallas import tpu as pltpu
from jax.sharding import PartitionSpec as P

LOADS = 8
ROWS = 24
SPRING = 0.5
SPLIT = 16
GROUP = 8
VMEM_LIMIT = 48 * 1024 * 1024

VMEM = pl.BlockSpec(memory_space=pltpu.VMEM)
SMEM = pl.BlockSpec(memory_space=pltpu.SMEM)
PARAMS = pltpu.CompilerParams(vmem_limit_bytes=VMEM_LIMIT)

_d, _l, _m = np.meshgrid(np.arange(8), np.arange(8), np.arange(8), indexing="ij")
DIAGONALS = ((_m - _l) % 8 == _d).astype(np.float32)


def to_diagonals(matrix):
    return jnp.sum(DIAGONALS * matrix[None], axis=2)


def from_diagonals(diagonals):
    return jnp.sum(DIAGONALS * diagonals[:, None, :], axis=0)


def spread(matrices, width):
    stacked = jnp.stack([to_diagonals(m) for m in matrices])
    return jnp.broadcast_to(stacked[..., None], stacked.shape + (width,))


def pack_kernel(shares, owner_ref, live_ref, force_ref, voxel_ref, near_ref, far_ref, count_ref):
    blocks = owner_ref.shape[0]
    devices, _, _, width = near_ref.shape
    empty = jnp.full((8, width), -1.0, jnp.float32)
    zero = jnp.zeros((8, width), jnp.float32)

    def clear(dev, carry):
        count_ref[dev] = 0
        for out_ref, share in zip((near_ref, far_ref), shares):
            for row in range(out_ref.shape[1]):
                out_ref[dev, row] = zero if row < 3 * share else empty
        return carry

    lax.fori_loop(0, devices, clear, 0)
    lane = lax.broadcasted_iota(jnp.int32, (8, width), 1)
    sub = lax.broadcasted_iota(jnp.int32, (8, width), 0)

    def place(block, carry):
        owner = owner_ref[block]
        rank = count_ref[owner]
        count_ref[owner] = rank + 1
        limit = jnp.full((8, width), live_ref[block, 0], jnp.int32)
        for load in range(1, LOADS):
            limit = jnp.where(sub == load, live_ref[block, load], limit)
        keep = lane < limit
        values = [
            jnp.where(keep, force_ref[block, k * 8 : k * 8 + 8, :], 0.0) for k in range(3)
        ]
        ids = voxel_ref[pl.ds(block, 1), :].astype(jnp.float32)

        def store(out_ref, share, slot):
            for k in range(3):
                out_ref[owner, slot * 3 + k] = values[k]
            out_ref[owner, 3 * share + slot // 8, pl.ds(slot % 8, 1), :] = ids

        @pl.when(rank < shares[0])
        def _():
            store(near_ref, shares[0], rank)

        @pl.when(rank >= shares[0])
        def _():
            store(far_ref, shares[1], rank - shares[0])

        return carry

    lax.fori_loop(0, blocks, place, 0)


def pack(owner, live, force, voxel, devices, shares):
    return pl.pallas_call(
        functools.partial(pack_kernel, shares),
        out_shape=tuple(
            jax.ShapeDtypeStruct((devices, 3 * c + -(-c // 8), 8, force.shape[2]), jnp.float32)
            for c in shares
        ),
        in_specs=[SMEM, SMEM, VMEM, VMEM],
        out_specs=(VMEM, VMEM),
        scratch_shapes=[pltpu.SMEM((devices,), jnp.int32)],
        compiler_params=PARAMS,
    )(owner, live, force, voxel)


def scatter_kernel(capacity, valid_ref, got_ref, *refs):
    before_ref = refs[0] if len(refs) == 5 else None
    out_ref, left_ref, acc_ref, list_ref = refs[-4:]
    devices, rows, _, width = got_ref.shape
    total = devices * capacity
    slots = GROUP * width
    cols = acc_ref.shape[2]
    tiles = acc_ref.shape[0]

    def gather(block, count):
        list_ref[count] = block
        return count + (valid_ref[block] > 0).astype(jnp.int32)

    count = lax.fori_loop(0, total, gather, jnp.int32(0))

    def clear(tile, carry):
        acc_ref[tile] = jnp.zeros(acc_ref.shape[1:], jnp.float32)
        return carry

    lax.fori_loop(0, tiles, clear, 0)
    column = lax.broadcasted_iota(jnp.int32, (cols, slots), 0)

    def step(index, carry):
        parts = []
        ids = []
        for j in range(GROUP):
            place = index * GROUP + j
            block = list_ref[jnp.where(place < count, place, 0)]
            dev = block // capacity
            slot = block % capacity
            parts.append(
                jnp.concatenate([got_ref[dev, slot * 3 + k] for k in range(3)], axis=0)
            )
            row = got_ref[dev, 3 * capacity + slot // 8, pl.ds(slot % 8, 1), :]
            ids.append(jnp.where(place < count, row, -1.0))
        values = jnp.concatenate(parts, axis=1)
        voxel = jnp.concatenate(ids, axis=1).astype(jnp.int32)
        high = values.astype(jnp.bfloat16).astype(jnp.float32)
        low = values - high
        both = jnp.concatenate([high, low], axis=0)
        line = lax.shift_right_arithmetic(voxel, 10)
        along = jnp.bitwise_and(voxel, tiles * cols - 1)
        for r in range(SPLIT):
            left_ref[r * 48 : r * 48 + 48, :] = jnp.where(line == r, both, 0.0).astype(
                jnp.bfloat16
            )

        def tile(t, inner):
            right = jnp.where(column == along - t * cols, 1.0, 0.0).astype(jnp.bfloat16)
            acc_ref[t] += lax.dot_general(
                left_ref[...],
                right,
                (((1,), (1,)), ((), ())),
                preferred_element_type=jnp.float32,
            )
            return inner

        lax.fori_loop(0, tiles, tile, 0, unroll=True)
        return carry

    lax.fori_loop(0, (count + GROUP - 1) // GROUP, step, 0)
    for r in range(SPLIT):
        for t in range(tiles):
            high = acc_ref[t, r * 48 : r * 48 + 24, :]
            result = high + acc_ref[t, r * 48 + 24 : r * 48 + 48, :]
            if before_ref is not None:
                result = result + before_ref[r * tiles + t]
            out_ref[r * tiles + t] = result


def scatter(got, capacity, depth, height, width_x, before=None):
    volume = depth * height * width_x
    tiles = volume // SPLIT // width_x
    assert volume // SPLIT == 1024
    first = got[:, 3 * capacity :, :, 0].reshape(got.shape[0], -1)[:, :capacity]
    valid = (first >= 0.0).astype(jnp.int32).reshape(-1)
    arrays = (valid, got) if before is None else (valid, got, before)
    slots = got.shape[0] * capacity * got.shape[3]
    return pl.pallas_call(
        functools.partial(scatter_kernel, capacity),
        out_shape=jax.ShapeDtypeStruct((depth * height, ROWS, width_x), jnp.float32),
        in_specs=[SMEM] + [VMEM] * (len(arrays) - 1),
        out_specs=VMEM,
        cost_estimate=pl.CostEstimate(
            flops=4 * SPLIT * 48 * 1024 * slots, bytes_accessed=4 * got.size, transcendentals=0
        ),
        scratch_shapes=[
            pltpu.VMEM((SPLIT * 48, GROUP * got.shape[3]), jnp.bfloat16),
            pltpu.VMEM((tiles, SPLIT * 48, width_x), jnp.float32),
            pltpu.SMEM((valid.shape[0] + 1,), jnp.int32),
        ],
        compiler_params=PARAMS,
    )(*arrays)


def shift_left(value):
    width = value.shape[-1]
    lane = lax.broadcasted_iota(jnp.int32, value.shape, 1)
    return jnp.where(lane == width - 1, 0.0, pltpu.roll(value, width - 1, 1))


def shift_right(value):
    lane = lax.broadcasted_iota(jnp.int32, value.shape, 1)
    return jnp.where(lane == 0, 0.0, pltpu.roll(value, 1, 1))


def mixed(*terms):
    width = terms[0][1][0].shape[1]
    columns = []
    for h in range(0, terms[0][0].shape[1], width):
        parts = []
        for k in range(3):
            total = None
            for s in range(8):
                product = None
                for value, coefficients in terms:
                    piece = value[k * 8 : k * 8 + 8, h : h + width] * coefficients[s]
                    product = piece if product is None else product + piece
                total = product if s == 0 else total + pltpu.roll(product, s, 0)
            parts.append(total)
        columns.append(jnp.concatenate(parts, axis=0))
    return jnp.concatenate(columns, axis=1)


def store_split(split_ref, z, y, value):
    both = jnp.concatenate([value, shift_left(value)], axis=0)
    high = both.astype(jnp.bfloat16)
    low = (both - high.astype(jnp.float32)).astype(jnp.bfloat16)
    split_ref[z, y, 0:48, :] = high
    split_ref[z, y, 48:96, :] = low


def run_operator(split_ref, field, weight_ref, matrix_ref, out_ref, carry_ref):
    planes, lines = split_ref.shape[0] - 1, split_ref.shape[1] - 1
    matrix = matrix_ref[...]

    def plane(ze, carry):
        weights = weight_ref[ze]
        before = None
        for ye in range(lines):
            corners = [split_ref.at[ze + a, ye + b] for a in (0, 1) for b in (0, 1)]
            high = jnp.concatenate([c[0:48, :] for c in corners], axis=0)
            low = jnp.concatenate([c[48:96, :] for c in corners], axis=0)
            forces = jnp.dot(
                matrix,
                jnp.concatenate([high, high, low], axis=0),
                preferred_element_type=jnp.float32,
            )
            forces = forces * weights[ye : ye + 1, :]
            if ye > 0:
                n = ye - 1
                lower = forces[0:48] + before[48:96] + carry_ref[n]
                carry_ref[n] = forces[96:144] + before[144:192]
                result = lower[0:24] + shift_right(lower[24:48])
                out_ref[ze, n] = result + SPRING * field(ze, ye)
            before = forces
        return carry

    carry_ref[...] = jnp.zeros(carry_ref.shape, jnp.float32)
    lax.fori_loop(0, planes, plane, 0)


def run_grams(first, second, depth, height, gram_ref):
    width = gram_ref.shape[1]

    def plane(z, carry):
        sums = list(carry)
        for y in range(height):
            a = first(z, y)
            b = second(z, y)
            for k in range(3):
                a8 = a[k * 8 : k * 8 + 8]
                b8 = b[k * 8 : k * 8 + 8]
                for s in range(8):
                    rolled = a8 if s == 0 else pltpu.roll(a8, s, 0)
                    for h in range(0, a8.shape[1], width):
                        sums[s] = sums[s] + rolled[:, h : h + width] * a8[:, h : h + width]
                        sums[8 + s] = sums[8 + s] + rolled[:, h : h + width] * b8[:, h : h + width]
        return tuple(sums)

    sums = lax.fori_loop(0, depth, plane, tuple(jnp.zeros((8, width), jnp.float32) for _ in range(16)))
    lane = lax.broadcasted_iota(jnp.int32, (8, width), 1)
    tile = jnp.zeros((8, width), jnp.float32)
    for s in range(16):
        tile = jnp.where(lane == s, jnp.sum(sums[s], axis=1, keepdims=True), tile)
    gram_ref[...] = tile


def first_kernel(field_ref, weight_ref, matrix_ref, out_ref, gram_ref, split_ref, carry_ref):
    depth, lines = field_ref.shape[0], field_ref.shape[1]

    def split(z, carry):
        for y in range(lines):
            store_split(split_ref, z, y, field_ref[z, y])
        return carry

    lax.fori_loop(0, depth, split, 0)
    run_operator(
        split_ref, lambda z, y: field_ref[z, y], weight_ref, matrix_ref, out_ref, carry_ref
    )
    run_grams(
        lambda z, y: field_ref[z + 1, y + 1],
        lambda z, y: out_ref[z + 1, y],
        depth - 2,
        lines - 2,
        gram_ref,
    )


def second_kernel(
    coef_ref, field_ref, applied_ref, weight_ref, matrix_ref,
    res_ref, out_ref, gram_ref, split_ref, carry_ref, full_ref,
):
    depth, lines = full_ref.shape[0], full_ref.shape[1]

    def split(z, carry):
        coef = [coef_ref[0, s] for s in range(8)]
        for y in range(lines):
            value = field_ref[z, y] - mixed((applied_ref[z, y], coef))
            full_ref[z, y] = value
            store_split(split_ref, z, y, value)
        return carry

    lax.fori_loop(0, depth, split, 0)
    run_operator(
        split_ref, lambda z, y: full_ref[z, y], weight_ref, matrix_ref, out_ref, carry_ref
    )
    run_grams(
        lambda z, y: full_ref[z + 1, y + 1],
        lambda z, y: out_ref[z + 1, y],
        depth - 2,
        lines - 2,
        gram_ref,
    )

    def keep(z, carry):
        for y in range(lines - 2):
            res_ref[z, y] = full_ref[z + 1, y + 1]
        return carry

    lax.fori_loop(0, depth - 2, keep, 0)


def last_kernel(coef_ref, field_ref, res_ref, first_ref, second_ref, disp_ref, out_ref):
    depth, lines = res_ref.shape[0], res_ref.shape[1]

    def plane(z, carry):
        coefs = [[coef_ref[i, s] for s in range(8)] for i in range(3)]
        for y in range(lines):
            residual = res_ref[z, y]
            disp = mixed((field_ref[z + 1, y + 1], coefs[0]), (residual, coefs[1]))
            left = residual - mixed(
                (second_ref[z + 1, y], coefs[1]), (first_ref[z + 1, y], coefs[2])
            )
            disp_ref[:, z, y, :] = disp
            out_ref[:, z, y, :] = left
        return carry

    lax.fori_loop(0, depth, plane, 0)


def first_operator(field, weights, matrix):
    depth, lines, _, width = field.shape
    return pl.pallas_call(
        first_kernel,
        out_shape=(
            jax.ShapeDtypeStruct((depth - 1, lines - 2, ROWS, width), jnp.float32),
            jax.ShapeDtypeStruct((8, 128), jnp.float32),
        ),
        in_specs=[VMEM] * 3,
        out_specs=(VMEM, VMEM),
        scratch_shapes=[
            pltpu.VMEM((depth, lines, 96, width), jnp.bfloat16),
            pltpu.VMEM((lines - 2, 48, width), jnp.float32),
        ],
        compiler_params=PARAMS,
    )(field, weights, matrix)


def second_operator(coef, field, applied, weights, matrix):
    depth, lines, _, width = field.shape
    return pl.pallas_call(
        second_kernel,
        out_shape=(
            jax.ShapeDtypeStruct((depth - 2, lines - 2, ROWS, width), jnp.float32),
            jax.ShapeDtypeStruct((depth - 1, lines - 2, ROWS, width), jnp.float32),
            jax.ShapeDtypeStruct((8, 128), jnp.float32),
        ),
        in_specs=[VMEM] * 5,
        out_specs=(VMEM, VMEM, VMEM),
        scratch_shapes=[
            pltpu.VMEM((depth, lines, 96, width), jnp.bfloat16),
            pltpu.VMEM((lines - 2, 48, width), jnp.float32),
            pltpu.VMEM((depth, lines, ROWS, width), jnp.float32),
        ],
        compiler_params=PARAMS,
    )(coef, field, applied, weights, matrix)


def last_update(coef, field, residual, first, second):
    depth, lines, _, width = residual.shape
    shape = jax.ShapeDtypeStruct((ROWS, depth, lines, width), jnp.float32)
    return pl.pallas_call(
        last_kernel,
        out_shape=(shape, shape),
        in_specs=[VMEM] * 5,
        out_specs=(VMEM, VMEM),
        compiler_params=PARAMS,
    )(coef, field, residual, first, second)


def with_below(block, axis, dim, below):
    count = lax.axis_size(axis)
    forward = [(i, i + 1) for i in range(count - 1)]
    size = block.shape[dim]
    low = lax.ppermute(lax.slice_in_dim(block, size - below, None, axis=dim), axis, forward)
    return jnp.concatenate([low, block], axis=dim)


def solve_small(matrix, target):
    factor = jnp.linalg.cholesky(matrix)
    halfway = lax.linalg.triangular_solve(factor, target, left_side=True, lower=True)
    return lax.linalg.triangular_solve(
        factor, halfway, left_side=True, lower=True, transpose_a=True
    )


HALO = 1
MESH = pl.DeviceIdType.MESH
WAYS = [(dz, dy) for dz in (-1, 0, 1) for dy in (-1, 0, 1) if (dz, dy) != (0, 0)]


def exists(counts, dz, dy):
    z, y = lax.axis_index("gz") + dz, lax.axis_index("gy") + dy
    return (z >= 0) & (z < counts[0]) & (y >= 0) & (y < counts[1])


def greet(counts, ways, peers):
    gz, gy = lax.axis_index("gz"), lax.axis_index("gy")
    barrier = pltpu.get_barrier_semaphore()
    for peer in peers:
        pl.semaphore_signal(barrier, inc=1, device_id=peer, device_id_type=MESH)
    total = jnp.int32(len(peers))
    for dz, dy in ways:
        total = total + jnp.where(exists(counts, dz, dy), 1, 0)

        @pl.when(exists(counts, dz, dy))
        def _():
            pl.semaphore_signal(barrier, inc=1, device_id=(gz + dz, gy + dy), device_id_type=MESH)

    pl.semaphore_wait(barrier, total)


class Halo:
    def __init__(self, counts, field_ref, first, out_ref, send_sems, recv_sems):
        self.counts, self.field, self.first, self.out = counts, field_ref, first, out_ref
        self.sems = (send_sems, recv_sems)
        self.depth, self.lines = field_ref.shape[0] - first, field_ref.shape[1]

    def source(self, step, size, first):
        low = first + {-1: 0, 0: 0, 1: size - HALO}[step]
        return pl.ds(low, size if step == 0 else HALO)

    def target(self, step, size):
        low = {-1: HALO + size, 0: HALO, 1: 0}[step]
        return pl.ds(low, size if step == 0 else HALO)

    def copy(self, i, sign):
        dz, dy = WAYS[i]
        return pltpu.make_async_remote_copy(
            src_ref=self.field.at[
                self.source(dz, self.depth, self.first), self.source(dy, self.lines, 0)
            ],
            dst_ref=self.out.at[self.target(dz, self.depth), self.target(dy, self.lines)],
            send_sem=self.sems[0].at[i],
            recv_sem=self.sems[1].at[i],
            device_id=(lax.axis_index("gz") + sign * dz, lax.axis_index("gy") + sign * dy),
            device_id_type=MESH,
        )

    def start(self):
        for i, (dz, dy) in enumerate(WAYS):

            @pl.when(exists(self.counts, dz, dy))
            def _():
                self.copy(i, 1).start()

    def fill(self):
        def keep(z, carry):
            for y in range(self.lines):
                self.out[z + HALO, y + HALO] = self.field[z + self.first, y]
            return carry

        lax.fori_loop(0, self.depth, keep, 0)
        zero = jnp.zeros(self.out.shape[2:], jnp.float32)
        for dz, dy in WAYS:

            @pl.when(jnp.logical_not(exists(self.counts, -dz, -dy)))
            def _():
                zs, ys = self.target(dz, self.depth), self.target(dy, self.lines)

                def clear(z, carry):
                    for y in range(ys.size):
                        self.out[zs.start + z, ys.start + y] = zero
                    return carry

                lax.fori_loop(0, zs.size, clear, 0)

    def finish(self):
        for i, (dz, dy) in enumerate(WAYS):

            @pl.when(exists(self.counts, dz, dy))
            def _():
                self.copy(i, 1).wait_send()

            @pl.when(exists(self.counts, -dz, -dy))
            def _():
                self.copy(i, -1).wait_recv()


def lines_of_peers(counts):
    gz, gy = lax.axis_index("gz"), lax.axis_index("gy")
    beside = [(gz, lax.rem(gy + d, counts[1])) for d in range(1, counts[1])]
    along = [(lax.rem(gz + d, counts[0]), gy) for d in range(1, counts[0])]
    return beside, along


def exchange(source_ref, slots_ref, place, peers, first, send_sems, recv_sems, meanwhile=None):
    copies = [
        pltpu.make_async_remote_copy(
            src_ref=source_ref,
            dst_ref=slots_ref.at[place],
            send_sem=send_sems.at[first + i],
            recv_sem=recv_sems.at[first + i],
            device_id=peer,
            device_id_type=MESH,
        )
        for i, peer in enumerate(peers)
    ]
    for copy in copies:
        copy.start()
    slots_ref[place] = source_ref[...]
    if meanwhile is not None:
        meanwhile()
    for copy in copies:
        copy.wait()
    total = slots_ref[0]
    for i in range(1, slots_ref.shape[0]):
        total = total + slots_ref[i]
    return total


def reduce_kernel(counts, tile_ref, out_ref, line_ref, plane_ref, mid_ref, send_sems, recv_sems):
    beside, along = lines_of_peers(counts)
    greet(counts, [], beside + along)
    sems = (send_sems, recv_sems)
    mid_ref[...] = exchange(tile_ref, line_ref, lax.axis_index("gy"), beside, 0, *sems)
    out_ref[...] = exchange(mid_ref, plane_ref, lax.axis_index("gz"), along, len(beside), *sems)


def reduce_halo_kernel(
    counts, tile_ref, field_ref, out_ref, full_ref,
    line_ref, plane_ref, mid_ref, send_sems, recv_sems, halo_send, halo_recv,
):
    beside, along = lines_of_peers(counts)
    greet(counts, [way for way in WAYS if 0 not in way], beside + along)
    sems = (send_sems, recv_sems)
    halo = Halo(counts, field_ref, 1, full_ref, halo_send, halo_recv)
    mid_ref[...] = exchange(tile_ref, line_ref, lax.axis_index("gy"), beside, 0, *sems)

    def meanwhile():
        halo.start()
        halo.fill()

    out_ref[...] = exchange(
        mid_ref, plane_ref, lax.axis_index("gz"), along, len(beside), *sems, meanwhile
    )
    halo.finish()


def reduce_scratch(tile):
    nz, ny = lax.axis_size("gz"), lax.axis_size("gy")
    return [
        pltpu.VMEM((ny,) + tile.shape, jnp.float32),
        pltpu.VMEM((nz,) + tile.shape, jnp.float32),
        pltpu.VMEM(tile.shape, jnp.float32),
        pltpu.SemaphoreType.DMA((ny + nz - 2,)),
        pltpu.SemaphoreType.DMA((ny + nz - 2,)),
    ]


HALO_SEMS = [pltpu.SemaphoreType.DMA((8,)), pltpu.SemaphoreType.DMA((8,))]


def remote(number):
    return pltpu.CompilerParams(
        collective_id=number, has_side_effects=True, vmem_limit_bytes=VMEM_LIMIT
    )


def grams_of(tile):
    sums = tile[:, :16].T
    return from_diagonals(sums[:8]), from_diagonals(sums[8:])


def total_grams(tile):
    counts = (lax.axis_size("gz"), lax.axis_size("gy"))
    sums = pl.pallas_call(
        functools.partial(reduce_kernel, counts),
        out_shape=jax.ShapeDtypeStruct(tile.shape, jnp.float32),
        in_specs=[VMEM],
        out_specs=VMEM,
        scratch_shapes=reduce_scratch(tile),
        compiler_params=remote(0),
    )(tile)
    return grams_of(sums)


def padded_shape(depth, lines, rows, width):
    return jax.ShapeDtypeStruct((depth + 2 * HALO, lines + 2 * HALO, rows, width), jnp.float32)


def total_grams_with_halo(tile, field):
    counts = (lax.axis_size("gz"), lax.axis_size("gy"))
    depth, lines, rows, width = field.shape
    sums, full = pl.pallas_call(
        functools.partial(reduce_halo_kernel, counts),
        out_shape=(
            jax.ShapeDtypeStruct(tile.shape, jnp.float32),
            padded_shape(depth - 1, lines, rows, width),
        ),
        in_specs=[VMEM, VMEM],
        out_specs=(VMEM, VMEM),
        scratch_shapes=reduce_scratch(tile) + HALO_SEMS,
        compiler_params=remote(2),
    )(tile, field)
    return grams_of(sums) + (full,)


def halo_kernel(counts, field_ref, out_ref, send_sems, recv_sems):
    greet(counts, WAYS, [])
    halo = Halo(counts, field_ref, 0, out_ref, send_sems, recv_sems)
    halo.start()
    halo.fill()
    halo.finish()


def field_with_halo(field):
    counts = (lax.axis_size("gz"), lax.axis_size("gy"))
    return pl.pallas_call(
        functools.partial(halo_kernel, counts),
        out_shape=padded_shape(*field.shape),
        in_specs=[VMEM],
        out_specs=VMEM,
        scratch_shapes=HALO_SEMS,
        compiler_params=remote(1),
    )(field)


def send_packed(packed):
    flat = packed.reshape(packed.shape[0], -1, packed.shape[3])
    got = lax.all_to_all(flat, ("gz", "gy"), split_axis=0, concat_axis=0, tiled=True)
    return got.reshape(packed.shape)


def small_dot(a, b):
    return jnp.sum(a[:, :, None] * b[None, :, :], axis=1)


def body(patch_force, patch_owner, patch_voxel, patch_live, voxel_mask, element_matrix):
    depth, height, width = voxel_mask.shape
    groups_z = lax.axis_size("gz")
    groups_y = lax.axis_size("gy")
    devices = groups_z * groups_y
    blocks = patch_force.shape[0]
    capacity = max(2, (2 * blocks + devices - 1) // devices)

    shares = (capacity // 2, capacity - capacity // 2)
    near, far = pack(patch_owner, patch_live, patch_force, patch_voxel, devices, shares)
    near = send_packed(near)
    near, far = lax.optimization_barrier((near, far))
    far = send_packed(far)

    weights = with_below(voxel_mask, "gz", 0, 1)
    weights = with_below(weights, "gy", 1, 1).astype(jnp.float32)
    wide = jnp.kron(element_matrix, jnp.eye(LOADS, dtype=jnp.float32))
    high = wide.astype(jnp.bfloat16)
    low = (wide - lax.reduce_precision(wide, 8, 7)).astype(jnp.bfloat16)
    matrix = jnp.concatenate([high, low, high], axis=1)

    force = scatter(near, shares[0], depth, height, width)
    force = scatter(far, shares[1], depth, height, width, force)
    field = field_with_halo(force.reshape(depth, height, ROWS, width))

    applied, gram = first_operator(field, weights, matrix)
    norm_gram, curvature, around = total_grams_with_halo(gram, applied)
    curvature = 0.5 * (curvature + curvature.T)
    alpha = solve_small(curvature, norm_gram)

    residual, again, gram = second_operator(
        spread([alpha], 128), field, around, weights, matrix
    )
    norm_next, cross = total_grams(gram)
    beta = solve_small(norm_gram, norm_next)
    curvature = cross - small_dot(small_dot(beta.T, curvature), beta)
    curvature = 0.5 * (curvature + curvature.T)
    alpha_next = solve_small(curvature, norm_next)
    joint = small_dot(beta, alpha_next)

    coef = spread([alpha + joint, alpha_next, joint], 128)
    return last_update(coef, field, residual, applied, again)


def solution(mesh):
    placed = (
        P(("gz", "gy"), None, None),
        P(("gz", "gy")),
        P(("gz", "gy"), None),
        P(("gz", "gy"), None),
        P("gz", "gy", None),
        P(),
    )
    return jax.shard_map(
        body,
        mesh=mesh,
        in_specs=placed,
        out_specs=(P(None, "gz", "gy", None), P(None, "gz", "gy", None)),
        check_vma=False,
    )
```
